32 devices in a mesh: row: 8 (over y, x, core), col: 4 (over z).
Axes of the slice: x: 2, y: 2, z: 4, core: 2. Of those that a mesh axis runs over, the one named last changes fastest.
Arguments:
- block_tiles: bfloat16 [8, 4, 32, 128, 128], P('row', 'col'), may hold values from -1.1953125 to 1.1953125
- block_index: int32 [8, 4, 32, 2], P('row', 'col'), may hold values from -1 to 127, as said below
Outputs:
- product: bfloat16 [8, 4, 32, 128, 128], P('row', 'col')
The draws below stay inside these ranges and needn't reach their ends.
Inputs may be any that keep to these rules, and one draw needn't show every extreme that they name: `block_index`: block numbers run within one matrix. Positions of rows v > c hold only empty slots; v = c holds the 32 diagonal blocks of its region; v < c holds 32 blocks of its region, exactly one in each block row and in each block column of the region. Slots are all live or all empty at a position, in any order. In the symmetric matrix every block row has exactly one nonzero block in each region of 32 block columns, and the pattern is closed: if X(i,k) and X(i,j) are nonzero then so is X(k,j), so the blocks form 32 chains that each hold one block row of every region.
All inputs are finite; a program needn't handle non-finite values.
Results may differ from the reference program's by a relative error of at most 0.0023.
Values may be sent and summed in bfloat16 or wider, within the bound.
No kernel may reach another device: no remote copies, remote signals or barrier semaphores. Data moves between devices by JAX's collectives and lax.ppermute only.
A program may use at most 64 MiB of HBM per device.

```python
import jax
import jax.numpy as jnp
import numpy as np
from jax import lax

BS = 128
NBD = 32
STEPS = 4
N_ROW = 8
N_COL = 4


def draw_block_index(key, part):
    key = jax.random.fold_in(key, 7)
    systems = N_ROW // N_COL
    order_key = jax.random.fold_in(key, 1)
    slot_key = jax.random.fold_in(key, 2)
    subkeys = jax.random.split(order_key, systems * N_COL)
    orders = jax.vmap(lambda single: jax.random.permutation(single, NBD))(subkeys)
    orders = orders.reshape(systems, N_COL, NBD).astype(jnp.int32)
    region = jnp.arange(N_COL, dtype=jnp.int32)
    row_ids = region[None, :, None] * NBD + orders
    row_part = jnp.broadcast_to(row_ids[:, :, None, :], (systems, N_COL, N_COL, NBD))
    col_part = jnp.broadcast_to(row_ids[:, None, :, :], (systems, N_COL, N_COL, NBD))
    upper_half = (region[:, None] <= region[None, :])[None, :, :, None]
    row_part = jnp.where(upper_half, row_part, -1)
    col_part = jnp.where(upper_half, col_part, -1)
    stacked = jnp.stack([row_part, col_part], axis=-1).astype(jnp.int32)
    slot_keys = jax.random.split(slot_key, systems * N_COL * N_COL)
    shuffles = jax.vmap(lambda single: jax.random.permutation(single, NBD))(slot_keys)
    shuffles = shuffles.reshape(systems, N_COL, N_COL, NBD, 1).astype(jnp.int32)
    shuffles = jnp.broadcast_to(shuffles, stacked.shape)
    stacked = jnp.take_along_axis(stacked, shuffles, axis=3)
    return jnp.transpose(stacked, (1, 0, 2, 3, 4)).reshape(N_ROW, N_COL, NBD, 2).astype(jnp.int32)


def levels(stream_key, dims, cuts, smallest, high):
    level, own = 1.0, jax.random.fold_in(stream_key, 6)
    for position, blocks in cuts:
        steps = jnp.exp(jax.random.uniform(jax.random.fold_in(own, position), (blocks,), jnp.float32, smallest / len(cuts), high / len(cuts)))
        level = level * jnp.repeat(steps, dims[position] // blocks).reshape([-1 if axis == position else 1 for axis in range(len(dims))])
    return level


def noise(own_key, extent, scale, limit, cuts=(), kind=jnp.bfloat16):
    loudness = levels(own_key, extent, cuts, -0.22, 0.18) if cuts else 1.0
    drawn = jax.random.normal(own_key, extent, jnp.float32) * scale * loudness
    return jnp.minimum(jnp.maximum(drawn, -limit), limit).astype(kind)


def setup_inputs(seed: int = 0) -> dict:
    keys = jax.random.split(jax.random.key(seed), 3)
    block_tiles = noise(keys[0], (N_ROW, N_COL, NBD, BS, BS), 0.2, 1.1953125, ((0, 8), (1, 4)))
    block_index = draw_block_index(jax.random.fold_in(keys[2], 71), 0)
    return dict(block_tiles=block_tiles, block_index=block_index)


def assemble(own_tiles, own_index, mirror_tiles, mirror_index):
    own_valid = own_index[:, 0] >= 0
    on_diagonal = own_index[:, 0] == own_index[:, 1]
    widened = own_tiles.astype(jnp.float32)
    symmetric = ((widened + jnp.swapaxes(widened, 1, 2)) * 0.5).astype(own_tiles.dtype)
    own_kept = jnp.where(on_diagonal[:, None, None], symmetric, own_tiles)
    mirror_valid = (mirror_index[:, 0] >= 0) & (mirror_index[:, 0] != mirror_index[:, 1])
    flipped = jnp.swapaxes(mirror_tiles, 1, 2)
    zero_tiles = jnp.zeros_like(own_tiles)
    merged = jnp.where(own_valid[:, None, None], own_kept, jnp.where(mirror_valid[:, None, None], flipped, zero_tiles))
    swapped_index = mirror_index[:, ::-1]
    empty_index = jnp.full_like(own_index, -1)
    merged_index = jnp.where(own_valid[:, None], own_index, jnp.where(mirror_valid[:, None], swapped_index, empty_index))
    return merged, merged_index


def multiply(left_tiles, left_index, right_tiles, right_index, out_index, totals):
    target_row = out_index[:, 0]
    target_col = out_index[:, 1]
    left_match = (left_index[None, :, 0] == target_row[:, None]) & (target_row[:, None] >= 0)
    left_found = jnp.any(left_match, axis=1)
    left_slot = jnp.argmax(left_match.astype(jnp.int32), axis=1).astype(jnp.int32)
    inner_block = jnp.take(left_index[:, 1], left_slot)
    right_match = (right_index[None, :, 0] == inner_block[:, None]) & (right_index[None, :, 1] == target_col[:, None])
    right_found = jnp.any(right_match, axis=1)
    right_slot = jnp.argmax(right_match.astype(jnp.int32), axis=1).astype(jnp.int32)
    usable = left_found & right_found
    chosen_left = jnp.take(left_tiles, left_slot, axis=0).astype(jnp.float32)
    chosen_left = jnp.where(usable[:, None, None], chosen_left, jnp.zeros((), jnp.float32))
    chosen_right = jnp.take(right_tiles, right_slot, axis=0).astype(jnp.float32)
    return totals + jnp.einsum("uxy,uyz->uxz", chosen_left, chosen_right)


def region_of(block_tiles, block_index, matrix_id, first, second, systems):
    own_row = first * systems + matrix_id
    mirror_row = second * systems + matrix_id
    return assemble(block_tiles[own_row, second], block_index[own_row, second], block_tiles[mirror_row, first], block_index[mirror_row, first])


def reference(block_tiles, block_index):
    systems = N_ROW // N_COL
    listing = np.array([(m, a, b) for m in range(systems) for a in range(N_COL) for b in range(a, N_COL)], dtype=np.int32)

    def one_region(record):
        matrix_id = record[0]
        first = record[1]
        second = record[2]
        out_index = block_index[first * systems + matrix_id, second]
        totals = jnp.zeros((NBD, BS, BS), jnp.float32)
        for step_index in range(STEPS):
            middle = (first + second + step_index) % N_COL
            left_part = region_of(block_tiles, block_index, matrix_id, first, middle, systems)
            right_part = region_of(block_tiles, block_index, matrix_id, middle, second, systems)
            totals = multiply(left_part[0], left_part[1], right_part[0], right_part[1], out_index, totals)
        valid = out_index[:, 0] >= 0
        return jnp.where(valid[:, None, None], totals, jnp.zeros((), jnp.float32)).astype(jnp.bfloat16)

    results = lax.map(one_region, jnp.asarray(listing))
    grid_rows = listing[:, 1] * systems + listing[:, 0]
    grid_cols = listing[:, 2]
    product = jnp.zeros(block_tiles.shape, jnp.bfloat16)
    return product.at[grid_rows, grid_cols].set(results)
```

```python
import functools

import jax
import jax.numpy as jnp
from jax import lax
from jax.experimental import pallas as pl
from jax.experimental.pallas import tpu as pltpu
from jax.sharding import PartitionSpec as P

STEPS = 4
VMEM_LIMIT = 48 * 1024 * 1024
AXES = ("row", "col")


def kind_of(m):
    return m % 2


def device(groups, systems, v, z, m):
    return (v * systems + m) * groups + z


def hub_pairs(groups, systems, offset):
    ring = groups - 1
    pairs = []
    for k in range(ring):
        partner = (k + offset) % ring
        if 2 * offset == ring and partner < k:
            continue
        low, high = min(k, partner), max(k, partner)
        for m in range(systems):
            if kind_of(m) == 0:
                source, target = (k, ring), (low, high)
            else:
                source, target = (0, k + 1), (low + 1, high + 1)
            pairs.append((device(groups, systems, *source, m), device(groups, systems, *target, m)))
    return pairs


def find_slots(groups, systems, own_ref, hub_refs, table, slot_ref):
    slots = slot_ref.shape[0]
    v = lax.axis_index("row") // systems
    c = lax.axis_index("col")
    kind = kind_of(lax.axis_index("row") % systems)
    first = jnp.where(kind == 0, (groups - 1) * slots, 0)
    direct = jnp.where(kind == 0, c == groups - 1, v == 0)

    @pl.when((v <= c) & direct)
    def _():
        for s in range(slots):
            slot_ref[own_ref[1 - kind, s] - first] = s

    @pl.when(v > c)
    def _():
        for s in range(slots):
            slot_ref[s] = s

    @pl.when((v <= c) & jnp.logical_not(direct))
    def _():
        key = sum(hub[kind, 0] for hub in hub_refs) // slots
        side = jnp.where(key == v, 0, 1)
        start = key * slots
        for s in range(slots):
            block = sum(hub[kind, s] for hub in hub_refs)
            table[block - start] = sum(hub[1 - kind, s] for hub in hub_refs) - first
        for s in range(slots):
            slot_ref[table[own_ref[side, s] - start]] = s


def symmetric(tile):
    wide = tile.astype(jnp.float32)
    return ((wide + wide.T) * 0.5).astype(jnp.bfloat16)


def place_of(groups, kind, v, z):
    low = groups // 2
    if kind == 0:
        return z // low, v * low + z % low
    return v // low, ((1 - z // low) * low + v % low) * low + z % low


def devices_of(groups, systems, half, m):
    found = {}
    for v in range(groups):
        for z in range(groups):
            h, p = place_of(groups, kind_of(m), v, z)
            if h == half:
                found[p] = device(groups, systems, v, z, m)
    return [found[p] for p in sorted(found)]


def half_groups(groups, systems):
    return [devices_of(groups, systems, h, m) for h in range(2) for m in range(systems)]


def larger_half(m):
    return 1 - kind_of(m)


def cross_pairs(groups, systems, larger):
    pairs = []
    for m in range(systems):
        source = larger_half(m) if larger else 1 - larger_half(m)
        pairs += list(zip(devices_of(groups, systems, source, m), devices_of(groups, systems, 1 - source, m)))
    return pairs


def sent_places(groups, larger):
    low = groups // 2
    stored = [p for p in range(low * low) if p // low <= p % low]
    return list(range(low * low)) if larger else stored


def swap_in_half(value, groups, systems):
    return lax.all_to_all(
        value,
        AXES,
        split_axis=0,
        concat_axis=0,
        axis_index_groups=half_groups(groups, systems),
        tiled=True,
    )


def stage_kernel(tiles_ref, out_ref):
    out_ref[...] = tiles_ref[...]


def sort_kernel(groups, systems, hubs, *refs):
    own_ref, hub_refs, tiles_ref = refs[0], refs[1 : 1 + hubs], refs[1 + hubs]
    out_ref, slot_ref, table = refs[2 + hubs :]
    find_slots(groups, systems, own_ref, hub_refs, table, slot_ref)
    spans, share = out_ref.shape[:2]
    for g in range(spans):
        for q in range(share):
            out_ref[g, q] = tiles_ref[slot_ref[g * share + q]]


def split_square_kernel(groups, systems, near_ref, from_larger_ref, from_smaller_ref, out_ref, dense):
    low = groups // 2
    spans, share, width = near_ref.shape[:3]
    v, z = lax.axis_index("row") // systems, lax.axis_index("col")
    kind = kind_of(lax.axis_index("row") % systems)
    half = jnp.where(kind == 0, z, v) // low

    def at(i, j=None):
        return slice(i * width, (i + 1 if j is None else j) * width)

    def square(k, h):
        larger = h == 1 - k
        far_ref = from_smaller_ref if larger else from_larger_ref
        arrived = sent_places(groups, not larger)
        for q in range(share):
            for a in range(groups):
                for b in range(a, groups):
                    side, p = place_of(groups, k, a, b)
                    if side == h:
                        tile = near_ref[p, q]
                    elif p < spans // 2:
                        tile = far_ref[arrived.index(p), q]
                    else:
                        continue
                    if a == b:
                        dense[q, at(a), at(a)] = symmetric(tile)
                    else:
                        dense[q, at(a), at(b)] = tile
                        dense[q, at(b), at(a)] = tile.T
            if k == 0:
                rows, columns = (0, (h + 1) * low), (h * low, (h + 1) * low)
            else:
                rows, columns = (h * low, (h + 1) * low), (h * low, groups)
            product = jnp.dot(
                dense[q, at(*rows), :], dense[q, :, at(*columns)], preferred_element_type=jnp.float32
            ).astype(jnp.bfloat16)
            for a in range(*rows):
                for b in range(max(a, columns[0]), columns[1]):
                    out_ref[place_of(groups, k, a, b)[1], q] = product[at(a - rows[0]), at(b - columns[0])]

    for k in range(min(systems, 2)):
        for h in range(2):
            pl.when((kind == k) & (half == h))(functools.partial(square, k, h))


def unsort_kernel(systems, slot_ref, sorted_ref, out_ref):
    spans, share = sorted_ref.shape[:2]
    stored = lax.axis_index("row") // systems <= lax.axis_index("col")

    @pl.when(stored)
    def _():
        for g in range(spans):
            for q in range(share):
                out_ref[slot_ref[g * share + q]] = sorted_ref[g, q]

    @pl.when(jnp.logical_not(stored))
    def _():
        out_ref[...] = jnp.zeros_like(out_ref)


def split_plan(own_tiles, own_index, hubs, groups, systems):
    slots, width = own_tiles.shape[0], own_tiles.shape[1]
    spans = groups * groups // 2
    share = slots // spans
    smem = pl.BlockSpec(memory_space=pltpu.SMEM)
    vmem = pl.BlockSpec(memory_space=pltpu.VMEM)
    params = pltpu.CompilerParams(vmem_limit_bytes=VMEM_LIMIT)
    region = jax.ShapeDtypeStruct(own_tiles.shape, jnp.bfloat16)
    by_group = jax.ShapeDtypeStruct((spans, share, width, width), jnp.bfloat16)

    staged = pl.pallas_call(
        stage_kernel,
        out_shape=region,
        in_specs=[vmem],
        out_specs=vmem,
        compiler_params=params,
        cost_estimate=pl.CostEstimate(flops=0, bytes_accessed=4 * own_tiles.size, transcendentals=0),
        name="stage_tiles",
    )(own_tiles)

    by_label, slot = pl.pallas_call(
        functools.partial(sort_kernel, groups, systems, len(hubs)),
        out_shape=[by_group, jax.ShapeDtypeStruct((slots,), jnp.int32)],
        in_specs=[smem] * (1 + len(hubs)) + [vmem],
        out_specs=[vmem, smem],
        scratch_shapes=[pltpu.SMEM((slots,), jnp.int32)],
        compiler_params=params,
        name="sort_by_chain",
    )(own_index, *hubs, staged)

    near = swap_in_half(by_label, groups, systems)
    crossing = []
    for larger in (True, False):
        sent = jnp.concatenate([near[p : p + 1] for p in sent_places(groups, larger)])
        crossing.append(lax.ppermute(sent, AXES, cross_pairs(groups, systems, larger)))
    squares = pl.pallas_call(
        functools.partial(split_square_kernel, groups, systems),
        out_shape=by_group,
        in_specs=[vmem] * 3,
        out_specs=vmem,
        scratch_shapes=[pltpu.VMEM((share, groups * width, groups * width), jnp.bfloat16)],
        compiler_params=params,
        name="square_chains",
    )(near, *crossing)
    returned = swap_in_half(squares, groups, systems)

    return pl.pallas_call(
        functools.partial(unsort_kernel, systems),
        out_shape=region,
        in_specs=[smem, vmem],
        out_specs=vmem,
        compiler_params=params,
        name="back_to_slots",
    )(slot, returned)


def spread_sort_kernel(groups, systems, hubs, *refs):
    own_ref, hub_refs, tiles_ref = refs[0], refs[1 : 1 + hubs], refs[1 + hubs]
    sorted_ref, slot_ref, table = refs[2 + hubs :]
    slots = slot_ref.shape[0]
    find_slots(groups, systems, own_ref, hub_refs, table, slot_ref)

    def move(t, carry):
        sorted_ref[t] = tiles_ref[slot_ref[t]]
        return carry

    lax.fori_loop(0, slots, move, 0)


def spread_unsort_kernel(slot_ref, sorted_ref, out_ref):
    def move(t, carry):
        out_ref[slot_ref[t]] = sorted_ref[t]
        return carry

    lax.fori_loop(0, out_ref.shape[0], move, 0)


def spread_square_kernel(groups, systems, tiles_ref, out_ref, dense):
    per_owner, width = tiles_ref.shape[1], tiles_ref.shape[2]

    def piece(v, m, c):
        return (v * systems + m) * groups + c

    def at(i):
        return pl.ds(i * width if isinstance(i, int) else pl.multiple_of(i * width, width), width)

    def one_chain(m, q):
        for i in range(groups):
            dense[at(i), at(i)] = symmetric(tiles_ref[piece(i, m, i), q])
            for j in range(i + 1, groups):
                tile = tiles_ref[piece(i, m, j), q]
                dense[at(i), at(j)] = tile
                dense[at(j), at(i)] = tile.T

        def one_tile(p, carry):
            a, b = p // groups, p % groups
            total = jnp.zeros((width, width), jnp.float32)
            for s in range(STEPS):
                k = lax.rem(a + b + s, groups)
                total += jnp.dot(dense[at(a), at(k)], dense[at(k), at(b)], preferred_element_type=jnp.float32)
            out_ref[piece(a, m, b), q] = jnp.where(a <= b, total, 0.0).astype(jnp.bfloat16)
            return carry

        lax.fori_loop(0, groups * groups, one_tile, 0)

    for m in range(systems):
        for q in range(per_owner):
            one_chain(m, q)


def spread_plan(own_tiles, own_index, hubs, groups, systems):
    slots, width = own_tiles.shape[0], own_tiles.shape[1]
    devices = groups * groups * systems
    per_owner = -(-slots // devices)
    pieces = per_owner * devices
    smem = pl.BlockSpec(memory_space=pltpu.SMEM)
    vmem = pl.BlockSpec(memory_space=pltpu.VMEM)
    params = pltpu.CompilerParams(vmem_limit_bytes=VMEM_LIMIT)

    by_label, slot = pl.pallas_call(
        functools.partial(spread_sort_kernel, groups, systems, len(hubs)),
        out_shape=(
            jax.ShapeDtypeStruct((slots, width, width), jnp.bfloat16),
            jax.ShapeDtypeStruct((slots,), jnp.int32),
        ),
        in_specs=[smem] * (1 + len(hubs)) + [vmem],
        out_specs=(vmem, smem),
        scratch_shapes=[pltpu.SMEM((slots,), jnp.int32)],
        compiler_params=params,
        name="sort_by_chain",
    )(own_index, *hubs, own_tiles)

    if pieces > slots:
        by_label = jnp.concatenate([by_label, jnp.zeros((pieces - slots, width, width), jnp.bfloat16)])
    outgoing = by_label.reshape(devices, per_owner, width, width)
    chains = lax.all_to_all(outgoing, AXES, split_axis=0, concat_axis=0, tiled=True)
    squares = pl.pallas_call(
        functools.partial(spread_square_kernel, groups, systems),
        out_shape=jax.ShapeDtypeStruct(chains.shape, jnp.bfloat16),
        in_specs=[vmem],
        out_specs=vmem,
        scratch_shapes=[pltpu.VMEM((groups * width, groups * width), jnp.bfloat16)],
        compiler_params=params,
        name="square_chains",
    )(chains)
    returned = lax.all_to_all(squares, AXES, split_axis=0, concat_axis=0, tiled=True)

    return pl.pallas_call(
        spread_unsort_kernel,
        out_shape=jax.ShapeDtypeStruct((slots, width, width), jnp.bfloat16),
        in_specs=[smem, vmem],
        out_specs=vmem,
        compiler_params=params,
        name="back_to_slots",
    )(slot, returned.reshape(pieces, width, width)[:slots])


def on_device(block_tiles, block_index):
    groups = lax.axis_size("col")
    systems = lax.axis_size("row") // groups
    own_tiles = block_tiles[0, 0]
    own_index = block_index[0, 0].T
    slots = own_tiles.shape[0]
    spans = groups * groups // 2

    hubs = [lax.ppermute(own_index, AXES, hub_pairs(groups, systems, offset)) for offset in reversed(range((groups + 1) // 2))]
    whole_window = groups == STEPS and slots % spans == 0
    plan = split_plan if whole_window else spread_plan
    return plan(own_tiles, own_index, hubs, groups, systems)[None, None]


def solution(mesh):
    in_specs = (P("row", "col", None, None, None), P("row", "col", None, None))
    out_specs = P("row", "col", None, None, None)
    return jax.shard_map(
        on_device, mesh=mesh, in_specs=in_specs, out_specs=out_specs, check_vma=False
    )
```

```python
import functools

import jax
import jax.numpy as jnp
from jax import lax
from jax.experimental import pallas as pl
from jax.experimental.pallas import tpu as pltpu
from jax.sharding import PartitionSpec as P

STEPS = 4
VMEM_LIMIT = 48 * 1024 * 1024
AXES = ("row", "col")


def kind_of(m):
    return m % 2


def device(groups, systems, v, z, m):
    return (v * systems + m) * groups + z


def hub_pairs(groups, systems, offset):
    ring = groups - 1
    pairs = []
    for k in range(ring):
        partner = (k + offset) % ring
        if 2 * offset == ring and partner < k:
            continue
        low, high = min(k, partner), max(k, partner)
        for m in range(systems):
            if kind_of(m) == 0:
                source, target = (k, ring), (low, high)
            else:
                source, target = (0, k + 1), (low + 1, high + 1)
            pairs.append((device(groups, systems, *source, m), device(groups, systems, *target, m)))
    return pairs


def find_slots(groups, systems, own_ref, hub_refs, table, slot_ref):
    slots = slot_ref.shape[0]
    v = lax.axis_index("row") // systems
    c = lax.axis_index("col")
    kind = kind_of(lax.axis_index("row") % systems)
    first = jnp.where(kind == 0, (groups - 1) * slots, 0)
    direct = jnp.where(kind == 0, c == groups - 1, v == 0)

    @pl.when((v <= c) & direct)
    def _():
        for s in range(slots):
            slot_ref[own_ref[1 - kind, s] - first] = s

    @pl.when(v > c)
    def _():
        for s in range(slots):
            slot_ref[s] = s

    @pl.when((v <= c) & jnp.logical_not(direct))
    def _():
        key = sum(hub[kind, 0] for hub in hub_refs) // slots
        side = jnp.where(key == v, 0, 1)
        start = key * slots
        for s in range(slots):
            block = sum(hub[kind, s] for hub in hub_refs)
            table[block - start] = sum(hub[1 - kind, s] for hub in hub_refs) - first
        for s in range(slots):
            slot_ref[table[own_ref[side, s] - start]] = s


def symmetric(tile):
    wide = tile.astype(jnp.float32)
    return ((wide + wide.T) * 0.5).astype(jnp.bfloat16)


def place_of(groups, kind, v, z):
    low = groups // 2
    return (z // low, v * low + z % low) if kind == 0 else (v // low, z * low + v % low)


def devices_of(groups, systems, half, m):
    found = {}
    for v in range(groups):
        for z in range(groups):
            h, p = place_of(groups, kind_of(m), v, z)
            if h == half:
                found[p] = device(groups, systems, v, z, m)
    return [found[p] for p in sorted(found)]


def half_groups(groups, systems):
    return [devices_of(groups, systems, h, m) for h in range(2) for m in range(systems)]


def line_groups(groups, systems):
    lines = []
    for m in range(systems):
        for fixed in range(groups):
            line = [(i, fixed) if kind_of(m) == 0 else (fixed, i) for i in range(groups)]
            lines.append([device(groups, systems, v, z, m) for v, z in line])
    return lines


def move_pairs(groups, systems, offset):
    pairs = []
    for m in range(systems):
        for v in range(groups):
            for z in range(groups):
                target = (v, z ^ offset) if kind_of(m) == 0 else (v ^ offset, z)
                pairs.append((device(groups, systems, v, z, m), device(groups, systems, *target, m)))
    return pairs


def swap(value, owners, members):
    shape = value.shape
    arrived = lax.all_to_all(
        value.reshape(owners, -1, *shape[1:]),
        AXES,
        split_axis=0,
        concat_axis=0,
        axis_index_groups=members,
        tiled=True,
    )
    return arrived.reshape(shape)


def stage_kernel(tiles_ref, out_ref):
    out_ref[...] = tiles_ref[...]


def sort_kernel(groups, systems, hubs, *refs):
    own_ref, hub_refs, tiles_ref = refs[0], refs[1 : 1 + hubs], refs[1 + hubs]
    out_ref, slot_ref, table = refs[2 + hubs :]
    find_slots(groups, systems, own_ref, hub_refs, table, slot_ref)
    for label in range(slot_ref.shape[0]):
        out_ref[label] = tiles_ref[slot_ref[label]]


def pick_kernel(groups, systems, near_ref, next_ref, far_ref, far_next_ref):
    low = groups // 2
    share = far_ref.shape[0] // low
    kind = kind_of(lax.axis_index("row") % systems)
    mine = lax.rem(jnp.where(kind == 0, lax.axis_index("col"), lax.axis_index("row") // systems), low)
    for source in range(groups):
        next_ref[source * share : (source + 1) * share] = near_ref[pl.ds((source * low + 1 - mine) * share, share)]
    for i in range(low):
        source = i + kind * low
        here = slice(i * share, (i + 1) * share)
        far_ref[here] = near_ref[pl.ds((source * low + mine) * share, share)]
        far_next_ref[here] = near_ref[pl.ds((source * low + 1 - mine) * share, share)]


def split_square_kernel(groups, systems, near_ref, next_ref, far_ref, far_next_ref, out_ref, dense):
    low = groups // 2
    spans = groups * low
    share, width = near_ref.shape[0] // spans, near_ref.shape[1]
    v, z = lax.axis_index("row") // systems, lax.axis_index("col")
    kind = kind_of(lax.axis_index("row") % systems)
    line = jnp.where(kind == 0, z, v)
    half, mine = line // low, lax.rem(line, low)

    def at(i, j=None):
        return slice(i * width, (i + 1 if j is None else j) * width)

    def tile_of(k, h, a, b, q):
        source, across = (a, b) if k == 0 else (b, a)
        if across // low == h:
            ours, theirs = near_ref[(source * low + mine) * share + q], next_ref[source * share + q]
        elif source // low == k:
            here = (source - k * low) * share + q
            ours, theirs = far_ref[here], far_next_ref[here]
        else:
            return None
        return jnp.where(mine == across % low, ours, theirs)

    def square(k, h):
        for q in range(share):
            for a in range(groups):
                for b in range(a, groups):
                    tile = tile_of(k, h, a, b, q)
                    if tile is None:
                        continue
                    if a == b:
                        dense[q, at(a), at(a)] = symmetric(tile)
                    else:
                        dense[q, at(a), at(b)] = tile
                        dense[q, at(b), at(a)] = tile.T
            if k == 0:
                rows, columns = (0, (h + 1) * low), (h * low, (h + 1) * low)
            else:
                rows, columns = (h * low, (h + 1) * low), (h * low, groups)
            product = jnp.dot(
                dense[q, at(*rows), :], dense[q, :, at(*columns)], preferred_element_type=jnp.float32
            ).astype(jnp.bfloat16)
            for a in range(*rows):
                for b in range(max(a, columns[0]), columns[1]):
                    place = place_of(groups, k, a, b)[1]
                    out_ref[place * share + q] = product[at(a - rows[0]), at(b - columns[0])]

    for k in sorted({kind_of(m) for m in range(systems)}):
        for h in range(2):
            pl.when((kind == k) & (half == h))(functools.partial(square, k, h))


def unsort_kernel(systems, slot_ref, sorted_ref, out_ref):
    stored = lax.axis_index("row") // systems <= lax.axis_index("col")

    @pl.when(stored)
    def _():
        for label in range(slot_ref.shape[0]):
            out_ref[slot_ref[label]] = sorted_ref[label]

    @pl.when(jnp.logical_not(stored))
    def _():
        out_ref[...] = jnp.zeros_like(out_ref)


def split_plan(own_tiles, own_index, hubs, groups, systems):
    slots, width = own_tiles.shape[0], own_tiles.shape[1]
    low = groups // 2
    spans = groups * low
    share = slots // spans
    smem = pl.BlockSpec(memory_space=pltpu.SMEM)
    vmem = pl.BlockSpec(memory_space=pltpu.VMEM)
    params = pltpu.CompilerParams(vmem_limit_bytes=VMEM_LIMIT)

    def tiles(count):
        return jax.ShapeDtypeStruct((count, width, width), jnp.bfloat16)

    staged = pl.pallas_call(
        stage_kernel,
        out_shape=tiles(slots),
        in_specs=[vmem],
        out_specs=vmem,
        compiler_params=params,
        cost_estimate=pl.CostEstimate(flops=0, bytes_accessed=4 * own_tiles.size, transcendentals=0),
        name="stage_tiles",
    )(own_tiles)

    by_label, slot = pl.pallas_call(
        functools.partial(sort_kernel, groups, systems, len(hubs)),
        out_shape=[tiles(slots), jax.ShapeDtypeStruct((slots,), jnp.int32)],
        in_specs=[smem] * (1 + len(hubs)) + [vmem],
        out_specs=[vmem, smem],
        scratch_shapes=[pltpu.SMEM((slots,), jnp.int32)],
        compiler_params=params,
        name="sort_by_chain",
    )(own_index, *hubs, staged)

    near = swap(by_label, groups, line_groups(groups, systems))
    moves = pl.pallas_call(
        functools.partial(pick_kernel, groups, systems),
        out_shape=[tiles(groups * share), tiles(low * share), tiles(low * share)],
        in_specs=[vmem],
        out_specs=[vmem] * 3,
        compiler_params=params,
        name="pick_moves",
    )(near)
    moved = [
        lax.ppermute(move, AXES, move_pairs(groups, systems, offset))
        for move, offset in zip(moves, (1, low, low + 1))
    ]
    squares = pl.pallas_call(
        functools.partial(split_square_kernel, groups, systems),
        out_shape=tiles(slots),
        in_specs=[vmem] * 4,
        out_specs=vmem,
        scratch_shapes=[pltpu.VMEM((share, groups * width, groups * width), jnp.bfloat16)],
        compiler_params=params,
        name="square_chains",
    )(near, *moved)
    returned = swap(squares, spans, half_groups(groups, systems))

    return pl.pallas_call(
        functools.partial(unsort_kernel, systems),
        out_shape=tiles(slots),
        in_specs=[smem, vmem],
        out_specs=vmem,
        compiler_params=params,
        name="back_to_slots",
    )(slot, returned)


def spread_sort_kernel(groups, systems, hubs, *refs):
    own_ref, hub_refs, tiles_ref = refs[0], refs[1 : 1 + hubs], refs[1 + hubs]
    sorted_ref, slot_ref, table = refs[2 + hubs :]
    slots = slot_ref.shape[0]
    find_slots(groups, systems, own_ref, hub_refs, table, slot_ref)

    def move(t, carry):
        sorted_ref[t] = tiles_ref[slot_ref[t]]
        return carry

    lax.fori_loop(0, slots, move, 0)


def spread_unsort_kernel(slot_ref, sorted_ref, out_ref):
    def move(t, carry):
        out_ref[slot_ref[t]] = sorted_ref[t]
        return carry

    lax.fori_loop(0, out_ref.shape[0], move, 0)


def spread_square_kernel(groups, systems, tiles_ref, out_ref, dense):
    per_owner, width = tiles_ref.shape[1], tiles_ref.shape[2]

    def piece(v, m, c):
        return (v * systems + m) * groups + c

    def at(i):
        return pl.ds(i * width if isinstance(i, int) else pl.multiple_of(i * width, width), width)

    def one_chain(m, q):
        for i in range(groups):
            dense[at(i), at(i)] = symmetric(tiles_ref[piece(i, m, i), q])
            for j in range(i + 1, groups):
                tile = tiles_ref[piece(i, m, j), q]
                dense[at(i), at(j)] = tile
                dense[at(j), at(i)] = tile.T

        def one_tile(p, carry):
            a, b = p // groups, p % groups
            total = jnp.zeros((width, width), jnp.float32)
            for s in range(STEPS):
                k = lax.rem(a + b + s, groups)
                total += jnp.dot(dense[at(a), at(k)], dense[at(k), at(b)], preferred_element_type=jnp.float32)
            out_ref[piece(a, m, b), q] = jnp.where(a <= b, total, 0.0).astype(jnp.bfloat16)
            return carry

        lax.fori_loop(0, groups * groups, one_tile, 0)

    for m in range(systems):
        for q in range(per_owner):
            one_chain(m, q)


def spread_plan(own_tiles, own_index, hubs, groups, systems):
    slots, width = own_tiles.shape[0], own_tiles.shape[1]
    devices = groups * groups * systems
    per_owner = -(-slots // devices)
    pieces = per_owner * devices
    smem = pl.BlockSpec(memory_space=pltpu.SMEM)
    vmem = pl.BlockSpec(memory_space=pltpu.VMEM)
    params = pltpu.CompilerParams(vmem_limit_bytes=VMEM_LIMIT)

    by_label, slot = pl.pallas_call(
        functools.partial(spread_sort_kernel, groups, systems, len(hubs)),
        out_shape=(
            jax.ShapeDtypeStruct((slots, width, width), jnp.bfloat16),
            jax.ShapeDtypeStruct((slots,), jnp.int32),
        ),
        in_specs=[smem] * (1 + len(hubs)) + [vmem],
        out_specs=(vmem, smem),
        scratch_shapes=[pltpu.SMEM((slots,), jnp.int32)],
        compiler_params=params,
        name="sort_by_chain",
    )(own_index, *hubs, own_tiles)

    if pieces > slots:
        by_label = jnp.concatenate([by_label, jnp.zeros((pieces - slots, width, width), jnp.bfloat16)])
    outgoing = by_label.reshape(devices, per_owner, width, width)
    chains = lax.all_to_all(outgoing, AXES, split_axis=0, concat_axis=0, tiled=True)
    squares = pl.pallas_call(
        functools.partial(spread_square_kernel, groups, systems),
        out_shape=jax.ShapeDtypeStruct(chains.shape, jnp.bfloat16),
        in_specs=[vmem],
        out_specs=vmem,
        scratch_shapes=[pltpu.VMEM((groups * width, groups * width), jnp.bfloat16)],
        compiler_params=params,
        name="square_chains",
    )(chains)
    returned = lax.all_to_all(squares, AXES, split_axis=0, concat_axis=0, tiled=True)

    return pl.pallas_call(
        spread_unsort_kernel,
        out_shape=jax.ShapeDtypeStruct((slots, width, width), jnp.bfloat16),
        in_specs=[smem, vmem],
        out_specs=vmem,
        compiler_params=params,
        name="back_to_slots",
    )(slot, returned.reshape(pieces, width, width)[:slots])


def on_device(block_tiles, block_index):
    groups = lax.axis_size("col")
    systems = lax.axis_size("row") // groups
    own_tiles = block_tiles[0, 0]
    own_index = block_index[0, 0].T
    slots = own_tiles.shape[0]
    spans = groups * groups // 2

    hubs = [lax.ppermute(own_index, AXES, hub_pairs(groups, systems, offset)) for offset in reversed(range((groups + 1) // 2))]
    whole_window = groups == STEPS and slots % spans == 0
    plan = split_plan if whole_window else spread_plan
    return plan(own_tiles, own_index, hubs, groups, systems)[None, None]


def solution(mesh):
    in_specs = (P("row", "col", None, None, None), P("row", "col", None, None))
    out_specs = P("row", "col", None, None, None)
    return jax.shard_map(
        on_device, mesh=mesh, in_specs=in_specs, out_specs=out_specs, check_vma=False
    )
```

```python
import functools

import jax
import jax.numpy as jnp
from jax import lax
from jax.experimental import pallas as pl
from jax.experimental.pallas import tpu as pltpu
from jax.sharding import PartitionSpec as P

STEPS = 4
VMEM_LIMIT = 48 * 1024 * 1024
AXES = ("row", "col")


def kind_of(m):
    return m % 2


def device(groups, systems, v, z, m):
    return (v * systems + m) * groups + z


def hub_pairs(groups, systems, turn):
    last = groups - 1
    pairs = []
    for m in range(systems):
        if kind_of(m) == 0:
            for v in range(last - turn if turn else last):
                target = (v, last - turn if turn else v)
                pairs.append((device(groups, systems, v, last, m), device(groups, systems, *target, m)))
        elif turn <= last // 2:
            for k in range(last):
                partner = (k + turn) % last
                if 2 * turn == last and partner < k:
                    continue
                target = (min(k, partner) + 1, max(k, partner) + 1)
                pairs.append((device(groups, systems, 0, k + 1, m), device(groups, systems, *target, m)))
    return pairs


def find_slots(groups, systems, own_ref, hub_refs, table, slot_ref):
    slots = slot_ref.shape[0]
    v = lax.axis_index("row") // systems
    c = lax.axis_index("col")
    kind = kind_of(lax.axis_index("row") % systems)
    first = jnp.where(kind == 0, (groups - 1) * slots, 0)
    direct = jnp.where(kind == 0, c == groups - 1, v == 0)

    @pl.when((v <= c) & direct)
    def _():
        for s in range(slots):
            slot_ref[own_ref[1 - kind, s] - first] = s

    @pl.when(v > c)
    def _():
        for s in range(slots):
            slot_ref[s] = s

    @pl.when((v <= c) & jnp.logical_not(direct))
    def _():
        key = sum(hub[kind, 0] for hub in hub_refs) // slots
        side = jnp.where(key == v, 0, 1)
        start = key * slots
        for s in range(slots):
            block = sum(hub[kind, s] for hub in hub_refs)
            table[block - start] = sum(hub[1 - kind, s] for hub in hub_refs) - first
        for s in range(slots):
            slot_ref[table[own_ref[side, s] - start]] = s


def symmetric(tile):
    wide = tile.astype(jnp.float32)
    return ((wide + wide.T) * 0.5).astype(jnp.bfloat16)


def place_of(groups, kind, v, z):
    low = groups // 2
    if kind == 0:
        half = z // low
        return half, v * low + (z % low if half else low - 1 - z)
    return v // low, ((1 - z // low) * low + v % low) * low + z % low


def devices_of(groups, systems, half, m):
    found = {}
    for v in range(groups):
        for z in range(groups):
            h, p = place_of(groups, kind_of(m), v, z)
            if h == half:
                found[p] = device(groups, systems, v, z, m)
    return [found[p] for p in sorted(found)]


def half_groups(groups, systems):
    return [devices_of(groups, systems, h, m) for h in range(2) for m in range(systems)]


def cross_pairs(groups, systems):
    pairs = []
    for m in range(systems):
        halves = [devices_of(groups, systems, h, m) for h in range(2)]
        pairs += list(zip(*halves)) + list(zip(*halves[::-1]))
    return pairs


def swap_in_half(value, groups, systems):
    return lax.all_to_all(
        value,
        AXES,
        split_axis=0,
        concat_axis=0,
        axis_index_groups=half_groups(groups, systems),
        tiled=True,
    )


def stage_kernel(tiles_ref, out_ref):
    out_ref[...] = tiles_ref[...]


def sort_kernel(groups, systems, hubs, *refs):
    own_ref, hub_refs, tiles_ref = refs[0], refs[1 : 1 + hubs], refs[1 + hubs]
    out_ref, slot_ref, table = refs[2 + hubs :]
    find_slots(groups, systems, own_ref, hub_refs, table, slot_ref)
    spans, share = out_ref.shape[:2]
    for g in range(spans):
        for q in range(share):
            out_ref[g, q] = tiles_ref[slot_ref[g * share + q]]


def split_square_kernel(groups, systems, near_ref, far_ref, out_ref, dense):
    low = groups // 2
    spans, share, width = near_ref.shape[:3]
    v, z = lax.axis_index("row") // systems, lax.axis_index("col")
    kind = kind_of(lax.axis_index("row") % systems)
    half = jnp.where(kind == 0, z, v) // low

    def at(i, j=None):
        return slice(i * width, (i + 1 if j is None else j) * width)

    def square(k, h):
        for q in range(share):
            for a in range(groups):
                for b in range(a, groups):
                    side, p = place_of(groups, k, a, b)
                    if side == h:
                        tile = near_ref[p, q]
                    elif p < spans // 2:
                        tile = far_ref[p, q]
                    else:
                        continue
                    if a == b:
                        dense[q, at(a), at(a)] = symmetric(tile)
                    else:
                        dense[q, at(a), at(b)] = tile
                        dense[q, at(b), at(a)] = tile.T
            if k == 0:
                rows, columns = (0, (h + 1) * low), (h * low, (h + 1) * low)
            else:
                rows, columns = (h * low, (h + 1) * low), (h * low, groups)
            product = jnp.dot(
                dense[q, at(*rows), :], dense[q, :, at(*columns)], preferred_element_type=jnp.float32
            ).astype(jnp.bfloat16)
            for a in range(*rows):
                for b in range(max(a, columns[0]), columns[1]):
                    out_ref[place_of(groups, k, a, b)[1], q] = product[at(a - rows[0]), at(b - columns[0])]

    for k in range(min(systems, 2)):
        for h in range(2):
            pl.when((kind == k) & (half == h))(functools.partial(square, k, h))


def unsort_kernel(systems, slot_ref, sorted_ref, out_ref):
    spans, share = sorted_ref.shape[:2]
    stored = lax.axis_index("row") // systems <= lax.axis_index("col")

    @pl.when(stored)
    def _():
        for g in range(spans):
            for q in range(share):
                out_ref[slot_ref[g * share + q]] = sorted_ref[g, q]

    @pl.when(jnp.logical_not(stored))
    def _():
        out_ref[...] = jnp.zeros_like(out_ref)


def split_plan(own_tiles, own_index, hubs, groups, systems):
    slots, width = own_tiles.shape[0], own_tiles.shape[1]
    spans = groups * groups // 2
    share = slots // spans
    smem = pl.BlockSpec(memory_space=pltpu.SMEM)
    vmem = pl.BlockSpec(memory_space=pltpu.VMEM)
    params = pltpu.CompilerParams(vmem_limit_bytes=VMEM_LIMIT)
    region = jax.ShapeDtypeStruct(own_tiles.shape, jnp.bfloat16)
    by_group = jax.ShapeDtypeStruct((spans, share, width, width), jnp.bfloat16)

    staged = pl.pallas_call(
        stage_kernel,
        out_shape=region,
        in_specs=[vmem],
        out_specs=vmem,
        compiler_params=params,
        cost_estimate=pl.CostEstimate(flops=0, bytes_accessed=4 * own_tiles.size, transcendentals=0),
        name="stage_tiles",
    )(own_tiles)

    by_label, slot = pl.pallas_call(
        functools.partial(sort_kernel, groups, systems, len(hubs)),
        out_shape=[by_group, jax.ShapeDtypeStruct((slots,), jnp.int32)],
        in_specs=[smem] * (1 + len(hubs)) + [vmem],
        out_specs=[vmem, smem],
        scratch_shapes=[pltpu.SMEM((slots,), jnp.int32)],
        compiler_params=params,
        name="sort_by_chain",
    )(own_index, *hubs, staged)

    near = swap_in_half(by_label, groups, systems)
    far = lax.ppermute(near[: spans // 2], AXES, cross_pairs(groups, systems))
    squares = pl.pallas_call(
        functools.partial(split_square_kernel, groups, systems),
        out_shape=by_group,
        in_specs=[vmem] * 2,
        out_specs=vmem,
        scratch_shapes=[pltpu.VMEM((share, groups * width, groups * width), jnp.bfloat16)],
        compiler_params=params,
        name="square_chains",
    )(near, far)
    returned = swap_in_half(squares, groups, systems)

    return pl.pallas_call(
        functools.partial(unsort_kernel, systems),
        out_shape=region,
        in_specs=[smem, vmem],
        out_specs=vmem,
        compiler_params=params,
        name="back_to_slots",
    )(slot, returned)


def spread_sort_kernel(groups, systems, hubs, *refs):
    own_ref, hub_refs, tiles_ref = refs[0], refs[1 : 1 + hubs], refs[1 + hubs]
    sorted_ref, slot_ref, table = refs[2 + hubs :]
    slots = slot_ref.shape[0]
    find_slots(groups, systems, own_ref, hub_refs, table, slot_ref)

    def move(t, carry):
        sorted_ref[t] = tiles_ref[slot_ref[t]]
        return carry

    lax.fori_loop(0, slots, move, 0)


def spread_unsort_kernel(slot_ref, sorted_ref, out_ref):
    def move(t, carry):
        out_ref[slot_ref[t]] = sorted_ref[t]
        return carry

    lax.fori_loop(0, out_ref.shape[0], move, 0)


def spread_square_kernel(groups, systems, tiles_ref, out_ref, dense):
    per_owner, width = tiles_ref.shape[1], tiles_ref.shape[2]

    def piece(v, m, c):
        return (v * systems + m) * groups + c

    def at(i):
        return pl.ds(i * width if isinstance(i, int) else pl.multiple_of(i * width, width), width)

    def one_chain(m, q):
        for i in range(groups):
            dense[at(i), at(i)] = symmetric(tiles_ref[piece(i, m, i), q])
            for j in range(i + 1, groups):
                tile = tiles_ref[piece(i, m, j), q]
                dense[at(i), at(j)] = tile
                dense[at(j), at(i)] = tile.T

        def one_tile(p, carry):
            a, b = p // groups, p % groups
            total = jnp.zeros((width, width), jnp.float32)
            for s in range(STEPS):
                k = lax.rem(a + b + s, groups)
                total += jnp.dot(dense[at(a), at(k)], dense[at(k), at(b)], preferred_element_type=jnp.float32)
            out_ref[piece(a, m, b), q] = jnp.where(a <= b, total, 0.0).astype(jnp.bfloat16)
            return carry

        lax.fori_loop(0, groups * groups, one_tile, 0)

    for m in range(systems):
        for q in range(per_owner):
            one_chain(m, q)


def spread_plan(own_tiles, own_index, hubs, groups, systems):
    slots, width = own_tiles.shape[0], own_tiles.shape[1]
    devices = groups * groups * systems
    per_owner = -(-slots // devices)
    pieces = per_owner * devices
    smem = pl.BlockSpec(memory_space=pltpu.SMEM)
    vmem = pl.BlockSpec(memory_space=pltpu.VMEM)
    params = pltpu.CompilerParams(vmem_limit_bytes=VMEM_LIMIT)

    by_label, slot = pl.pallas_call(
        functools.partial(spread_sort_kernel, groups, systems, len(hubs)),
        out_shape=(
            jax.ShapeDtypeStruct((slots, width, width), jnp.bfloat16),
            jax.ShapeDtypeStruct((slots,), jnp.int32),
        ),
        in_specs=[smem] * (1 + len(hubs)) + [vmem],
        out_specs=(vmem, smem),
        scratch_shapes=[pltpu.SMEM((slots,), jnp.int32)],
        compiler_params=params,
        name="sort_by_chain",
    )(own_index, *hubs, own_tiles)

    if pieces > slots:
        by_label = jnp.concatenate([by_label, jnp.zeros((pieces - slots, width, width), jnp.bfloat16)])
    outgoing = by_label.reshape(devices, per_owner, width, width)
    chains = lax.all_to_all(outgoing, AXES, split_axis=0, concat_axis=0, tiled=True)
    squares = pl.pallas_call(
        functools.partial(spread_square_kernel, groups, systems),
        out_shape=jax.ShapeDtypeStruct(chains.shape, jnp.bfloat16),
        in_specs=[vmem],
        out_specs=vmem,
        scratch_shapes=[pltpu.VMEM((groups * width, groups * width), jnp.bfloat16)],
        compiler_params=params,
        name="square_chains",
    )(chains)
    returned = lax.all_to_all(squares, AXES, split_axis=0, concat_axis=0, tiled=True)

    return pl.pallas_call(
        spread_unsort_kernel,
        out_shape=jax.ShapeDtypeStruct((slots, width, width), jnp.bfloat16),
        in_specs=[smem, vmem],
        out_specs=vmem,
        compiler_params=params,
        name="back_to_slots",
    )(slot, returned.reshape(pieces, width, width)[:slots])


def on_device(block_tiles, block_index):
    groups = lax.axis_size("col")
    systems = lax.axis_size("row") // groups
    own_tiles = block_tiles[0, 0]
    own_index = block_index[0, 0].T
    slots = own_tiles.shape[0]
    spans = groups * groups // 2

    hubs = [lax.ppermute(own_index, AXES, hub_pairs(groups, systems, turn)) for turn in reversed(range(groups - 1))]
    whole_window = groups == STEPS and slots % spans == 0
    plan = split_plan if whole_window else spread_plan
    return plan(own_tiles, own_index, hubs, groups, systems)[None, None]


def solution(mesh):
    in_specs = (P("row", "col", None, None, None), P("row", "col", None, None))
    out_specs = P("row", "col", None, None, None)
    return jax.shard_map(
        on_device, mesh=mesh, in_specs=in_specs, out_specs=out_specs, check_vma=False
    )
```

```python
import functools

import jax
import jax.numpy as jnp
from jax import lax
from jax.experimental import pallas as pl
from jax.experimental.pallas import tpu as pltpu
from jax.sharding import PartitionSpec as P

STEPS = 4
VMEM_LIMIT = 48 * 1024 * 1024
AXES = ("row", "col")


def kind_of(m):
    return m % 2


def device(groups, systems, v, z, m):
    return (v * systems + m) * groups + z


def hub_pairs(groups, systems, offset):
    ring = groups - 1
    pairs = []
    for k in range(ring):
        partner = (k + offset) % ring
        if 2 * offset == ring and partner < k:
            continue
        low, high = min(k, partner), max(k, partner)
        for m in range(systems):
            if kind_of(m) == 0:
                source, target = (k, ring), (low, high)
            else:
                source, target = (0, k + 1), (low + 1, high + 1)
            pairs.append((device(groups, systems, *source, m), device(groups, systems, *target, m)))
    return pairs


def find_slots(groups, systems, own_ref, hub_refs, table, slot_ref):
    slots = slot_ref.shape[0]
    v = lax.axis_index("row") // systems
    c = lax.axis_index("col")
    kind = kind_of(lax.axis_index("row") % systems)
    first = jnp.where(kind == 0, (groups - 1) * slots, 0)
    direct = jnp.where(kind == 0, c == groups - 1, v == 0)

    @pl.when((v <= c) & direct)
    def _():
        for s in range(slots):
            slot_ref[own_ref[1 - kind, s] - first] = s

    @pl.when(v > c)
    def _():
        for s in range(slots):
            slot_ref[s] = s

    @pl.when((v <= c) & jnp.logical_not(direct))
    def _():
        key = sum(hub[kind, 0] for hub in hub_refs) // slots
        side = jnp.where(key == v, 0, 1)
        start = key * slots
        for s in range(slots):
            block = sum(hub[kind, s] for hub in hub_refs)
            table[block - start] = sum(hub[1 - kind, s] for hub in hub_refs) - first
        for s in range(slots):
            slot_ref[table[own_ref[side, s] - start]] = s


def symmetric(tile):
    wide = tile.astype(jnp.float32)
    return ((wide + wide.T) * 0.5).astype(jnp.bfloat16)


def place_of(groups, kind, v, z):
    low = groups // 2
    if kind == 0:
        half = z // low
        return half, v * low + (z % low if half else low - 1 - z)
    half = v // low
    return half, ((1 - z // low) * low + (low - 1 - v % low if half else v)) * low + z % low


def devices_of(groups, systems, half, m):
    found = {}
    for v in range(groups):
        for z in range(groups):
            h, p = place_of(groups, kind_of(m), v, z)
            if h == half:
                found[p] = device(groups, systems, v, z, m)
    return [found[p] for p in sorted(found)]


def half_groups(groups, systems):
    return [devices_of(groups, systems, h, m) for h in range(2) for m in range(systems)]


def cross_pairs(groups, systems):
    pairs = []
    for m in range(systems):
        halves = [devices_of(groups, systems, h, m) for h in range(2)]
        pairs += list(zip(*halves)) + list(zip(*halves[::-1]))
    return pairs


def swap_in_half(value, groups, systems):
    return lax.all_to_all(
        value,
        AXES,
        split_axis=0,
        concat_axis=0,
        axis_index_groups=half_groups(groups, systems),
        tiled=True,
    )


def stage_kernel(tiles_ref, out_ref):
    out_ref[...] = tiles_ref[...]


def sort_kernel(groups, systems, hubs, *refs):
    own_ref, hub_refs, tiles_ref = refs[0], refs[1 : 1 + hubs], refs[1 + hubs]
    out_ref, slot_ref, table = refs[2 + hubs :]
    find_slots(groups, systems, own_ref, hub_refs, table, slot_ref)
    spans, share = out_ref.shape[:2]
    for g in range(spans):
        for q in range(share):
            out_ref[g, q] = tiles_ref[slot_ref[g * share + q]]


def split_square_kernel(groups, systems, near_ref, far_ref, out_ref, dense):
    low = groups // 2
    spans, share, width = near_ref.shape[:3]
    v, z = lax.axis_index("row") // systems, lax.axis_index("col")
    kind = kind_of(lax.axis_index("row") % systems)
    half = jnp.where(kind == 0, z, v) // low

    def at(i, j=None):
        return slice(i * width, (i + 1 if j is None else j) * width)

    def square(k, h):
        for q in range(share):
            for a in range(groups):
                for b in range(a, groups):
                    side, p = place_of(groups, k, a, b)
                    if side == h:
                        tile = near_ref[p, q]
                    elif p < spans // 2:
                        tile = far_ref[p, q]
                    else:
                        continue
                    if a == b:
                        dense[q, at(a), at(a)] = symmetric(tile)
                    else:
                        dense[q, at(a), at(b)] = tile
                        dense[q, at(b), at(a)] = tile.T
            if k == 0:
                rows, columns = (0, (h + 1) * low), (h * low, (h + 1) * low)
            else:
                rows, columns = (h * low, (h + 1) * low), (h * low, groups)
            product = jnp.dot(
                dense[q, at(*rows), :], dense[q, :, at(*columns)], preferred_element_type=jnp.float32
            ).astype(jnp.bfloat16)
            for a in range(*rows):
                for b in range(max(a, columns[0]), columns[1]):
                    out_ref[place_of(groups, k, a, b)[1], q] = product[at(a - rows[0]), at(b - columns[0])]

    for k in range(min(systems, 2)):
        for h in range(2):
            pl.when((kind == k) & (half == h))(functools.partial(square, k, h))


def unsort_kernel(systems, slot_ref, sorted_ref, out_ref):
    spans, share = sorted_ref.shape[:2]
    stored = lax.axis_index("row") // systems <= lax.axis_index("col")

    @pl.when(stored)
    def _():
        for g in range(spans):
            for q in range(share):
                out_ref[slot_ref[g * share + q]] = sorted_ref[g, q]

    @pl.when(jnp.logical_not(stored))
    def _():
        out_ref[...] = jnp.zeros_like(out_ref)


def split_plan(own_tiles, own_index, hubs, groups, systems):
    slots, width = own_tiles.shape[0], own_tiles.shape[1]
    spans = groups * groups // 2
    share = slots // spans
    smem = pl.BlockSpec(memory_space=pltpu.SMEM)
    vmem = pl.BlockSpec(memory_space=pltpu.VMEM)
    params = pltpu.CompilerParams(vmem_limit_bytes=VMEM_LIMIT)
    region = jax.ShapeDtypeStruct(own_tiles.shape, jnp.bfloat16)
    by_group = jax.ShapeDtypeStruct((spans, share, width, width), jnp.bfloat16)

    staged = pl.pallas_call(
        stage_kernel,
        out_shape=region,
        in_specs=[vmem],
        out_specs=vmem,
        compiler_params=params,
        cost_estimate=pl.CostEstimate(flops=0, bytes_accessed=4 * own_tiles.size, transcendentals=0),
        name="stage_tiles",
    )(own_tiles)

    by_label, slot = pl.pallas_call(
        functools.partial(sort_kernel, groups, systems, len(hubs)),
        out_shape=[by_group, jax.ShapeDtypeStruct((slots,), jnp.int32)],
        in_specs=[smem] * (1 + len(hubs)) + [vmem],
        out_specs=[vmem, smem],
        scratch_shapes=[pltpu.SMEM((slots,), jnp.int32)],
        compiler_params=params,
        name="sort_by_chain",
    )(own_index, *hubs, staged)

    near = swap_in_half(by_label, groups, systems)
    far = lax.ppermute(near[: spans // 2], AXES, cross_pairs(groups, systems))
    squares = pl.pallas_call(
        functools.partial(split_square_kernel, groups, systems),
        out_shape=by_group,
        in_specs=[vmem] * 2,
        out_specs=vmem,
        scratch_shapes=[pltpu.VMEM((share, groups * width, groups * width), jnp.bfloat16)],
        compiler_params=params,
        name="square_chains",
    )(near, far)
    returned = swap_in_half(squares, groups, systems)

    return pl.pallas_call(
        functools.partial(unsort_kernel, systems),
        out_shape=region,
        in_specs=[smem, vmem],
        out_specs=vmem,
        compiler_params=params,
        name="back_to_slots",
    )(slot, returned)


def spread_sort_kernel(groups, systems, hubs, *refs):
    own_ref, hub_refs, tiles_ref = refs[0], refs[1 : 1 + hubs], refs[1 + hubs]
    sorted_ref, slot_ref, table = refs[2 + hubs :]
    slots = slot_ref.shape[0]
    find_slots(groups, systems, own_ref, hub_refs, table, slot_ref)

    def move(t, carry):
        sorted_ref[t] = tiles_ref[slot_ref[t]]
        return carry

    lax.fori_loop(0, slots, move, 0)


def spread_unsort_kernel(slot_ref, sorted_ref, out_ref):
    def move(t, carry):
        out_ref[slot_ref[t]] = sorted_ref[t]
        return carry

    lax.fori_loop(0, out_ref.shape[0], move, 0)


def spread_square_kernel(groups, systems, tiles_ref, out_ref, dense):
    per_owner, width = tiles_ref.shape[1], tiles_ref.shape[2]

    def piece(v, m, c):
        return (v * systems + m) * groups + c

    def at(i):
        return pl.ds(i * width if isinstance(i, int) else pl.multiple_of(i * width, width), width)

    def one_chain(m, q):
        for i in range(groups):
            dense[at(i), at(i)] = symmetric(tiles_ref[piece(i, m, i), q])
            for j in range(i + 1, groups):
                tile = tiles_ref[piece(i, m, j), q]
                dense[at(i), at(j)] = tile
                dense[at(j), at(i)] = tile.T

        def one_tile(p, carry):
            a, b = p // groups, p % groups
            total = jnp.zeros((width, width), jnp.float32)
            for s in range(STEPS):
                k = lax.rem(a + b + s, groups)
                total += jnp.dot(dense[at(a), at(k)], dense[at(k), at(b)], preferred_element_type=jnp.float32)
            out_ref[piece(a, m, b), q] = jnp.where(a <= b, total, 0.0).astype(jnp.bfloat16)
            return carry

        lax.fori_loop(0, groups * groups, one_tile, 0)

    for m in range(systems):
        for q in range(per_owner):
            one_chain(m, q)


def spread_plan(own_tiles, own_index, hubs, groups, systems):
    slots, width = own_tiles.shape[0], own_tiles.shape[1]
    devices = groups * groups * systems
    per_owner = -(-slots // devices)
    pieces = per_owner * devices
    smem = pl.BlockSpec(memory_space=pltpu.SMEM)
    vmem = pl.BlockSpec(memory_space=pltpu.VMEM)
    params = pltpu.CompilerParams(vmem_limit_bytes=VMEM_LIMIT)

    by_label, slot = pl.pallas_call(
        functools.partial(spread_sort_kernel, groups, systems, len(hubs)),
        out_shape=(
            jax.ShapeDtypeStruct((slots, width, width), jnp.bfloat16),
            jax.ShapeDtypeStruct((slots,), jnp.int32),
        ),
        in_specs=[smem] * (1 + len(hubs)) + [vmem],
        out_specs=(vmem, smem),
        scratch_shapes=[pltpu.SMEM((slots,), jnp.int32)],
        compiler_params=params,
        name="sort_by_chain",
    )(own_index, *hubs, own_tiles)

    if pieces > slots:
        by_label = jnp.concatenate([by_label, jnp.zeros((pieces - slots, width, width), jnp.bfloat16)])
    outgoing = by_label.reshape(devices, per_owner, width, width)
    chains = lax.all_to_all(outgoing, AXES, split_axis=0, concat_axis=0, tiled=True)
    squares = pl.pallas_call(
        functools.partial(spread_square_kernel, groups, systems),
        out_shape=jax.ShapeDtypeStruct(chains.shape, jnp.bfloat16),
        in_specs=[vmem],
        out_specs=vmem,
        scratch_shapes=[pltpu.VMEM((groups * width, groups * width), jnp.bfloat16)],
        compiler_params=params,
        name="square_chains",
    )(chains)
    returned = lax.all_to_all(squares, AXES, split_axis=0, concat_axis=0, tiled=True)

    return pl.pallas_call(
        spread_unsort_kernel,
        out_shape=jax.ShapeDtypeStruct((slots, width, width), jnp.bfloat16),
        in_specs=[smem, vmem],
        out_specs=vmem,
        compiler_params=params,
        name="back_to_slots",
    )(slot, returned.reshape(pieces, width, width)[:slots])


def on_device(block_tiles, block_index):
    groups = lax.axis_size("col")
    systems = lax.axis_size("row") // groups
    own_tiles = block_tiles[0, 0]
    own_index = block_index[0, 0].T
    slots = own_tiles.shape[0]
    spans = groups * groups // 2

    hubs = [lax.ppermute(own_index, AXES, hub_pairs(groups, systems, offset)) for offset in reversed(range((groups + 1) // 2))]
    whole_window = groups == STEPS and slots % spans == 0
    plan = split_plan if whole_window else spread_plan
    return plan(own_tiles, own_index, hubs, groups, systems)[None, None]


def solution(mesh):
    in_specs = (P("row", "col", None, None, None), P("row", "col", None, None))
    out_specs = P("row", "col", None, None, None)
    return jax.shard_map(
        on_device, mesh=mesh, in_specs=in_specs, out_specs=out_specs, check_vma=False
    )
```

```python
import functools

import jax
import jax.numpy as jnp
from jax import lax
from jax.experimental import pallas as pl
from jax.experimental.pallas import tpu as pltpu
from jax.sharding import PartitionSpec as P

STEPS = 4
VMEM_LIMIT = 48 * 1024 * 1024
AXES = ("row", "col")


def kind_of(m):
    return m % 2


def device(groups, systems, v, z, m):
    return (v * systems + m) * groups + z


def hub_pairs(groups, systems, offset):
    ring = groups - 1
    pairs = []
    for k in range(ring):
        partner = (k + offset) % ring
        if 2 * offset == ring and partner < k:
            continue
        low, high = min(k, partner), max(k, partner)
        for m in range(systems):
            if kind_of(m) == 0:
                source, target = (k, ring), (low, high)
            else:
                source, target = (0, k + 1), (low + 1, high + 1)
            pairs.append((device(groups, systems, *source, m), device(groups, systems, *target, m)))
    return pairs


def find_slots(groups, systems, own_ref, hub_refs, table, slot_ref):
    slots = slot_ref.shape[0]
    v = lax.axis_index("row") // systems
    c = lax.axis_index("col")
    kind = kind_of(lax.axis_index("row") % systems)
    first = jnp.where(kind == 0, (groups - 1) * slots, 0)
    direct = jnp.where(kind == 0, c == groups - 1, v == 0)

    @pl.when((v <= c) & direct)
    def _():
        for s in range(slots):
            slot_ref[own_ref[1 - kind, s] - first] = s

    @pl.when(v > c)
    def _():
        for s in range(slots):
            slot_ref[s] = s

    @pl.when((v <= c) & jnp.logical_not(direct))
    def _():
        key = sum(hub[kind, 0] for hub in hub_refs) // slots
        side = jnp.where(key == v, 0, 1)
        start = key * slots
        for s in range(slots):
            block = sum(hub[kind, s] for hub in hub_refs)
            table[block - start] = sum(hub[1 - kind, s] for hub in hub_refs) - first
        for s in range(slots):
            slot_ref[table[own_ref[side, s] - start]] = s


def symmetric(tile):
    wide = tile.astype(jnp.float32)
    return ((wide + wide.T) * 0.5).astype(jnp.bfloat16)


def place_of(groups, kind, v, z):
    low = groups // 2
    if kind == 0:
        half = z // low
        return half, v * low + (z % low if half else low - 1 - z)
    return v // low, ((1 - z // low) * low + v % low) * low + z % low


def devices_of(groups, systems, half, m):
    found = {}
    for v in range(groups):
        for z in range(groups):
            h, p = place_of(groups, kind_of(m), v, z)
            if h == half:
                found[p] = device(groups, systems, v, z, m)
    return [found[p] for p in sorted(found)]


def half_groups(groups, systems):
    return [devices_of(groups, systems, h, m) for h in range(2) for m in range(systems)]


def cross_pairs(groups, systems):
    pairs = []
    for m in range(systems):
        halves = [devices_of(groups, systems, h, m) for h in range(2)]
        pairs += list(zip(*halves)) + list(zip(*halves[::-1]))
    return pairs


def swap_in_half(value, groups, systems):
    return lax.all_to_all(
        value,
        AXES,
        split_axis=0,
        concat_axis=0,
        axis_index_groups=half_groups(groups, systems),
        tiled=True,
    )


def stage_kernel(tiles_ref, out_ref):
    out_ref[...] = tiles_ref[...]


def sort_kernel(groups, systems, hubs, *refs):
    own_ref, hub_refs, tiles_ref = refs[0], refs[1 : 1 + hubs], refs[1 + hubs]
    out_ref, slot_ref, table = refs[2 + hubs :]
    find_slots(groups, systems, own_ref, hub_refs, table, slot_ref)
    spans, share = out_ref.shape[:2]
    for g in range(spans):
        for q in range(share):
            out_ref[g, q] = tiles_ref[slot_ref[g * share + q]]


def each_half(groups, systems, body):
    low = groups // 2
    v, z = lax.axis_index("row") // systems, lax.axis_index("col")
    kind = kind_of(lax.axis_index("row") % systems)
    half = jnp.where(kind == 0, z, v) // low
    for k in sorted({kind_of(m) for m in range(systems)}):
        for h in range(2):
            pl.when((kind == k) & (half == h))(functools.partial(body, k, h))


def fill(groups, k, h, own, tiles_ref, dense_ref):
    spans, share, width = groups * groups // 2, tiles_ref.shape[1], tiles_ref.shape[2]

    def at(i):
        return slice(i * width, (i + 1) * width)

    for q in range(share):
        for a in range(groups):
            for b in range(a, groups):
                side, p = place_of(groups, k, a, b)
                if (side == h) != own or (not own and p >= spans // 2):
                    continue
                tile = tiles_ref[p, q]
                if a == b:
                    dense_ref[q, at(a), at(a)] = symmetric(tile)
                else:
                    dense_ref[q, at(a), at(b)] = tile
                    dense_ref[q, at(b), at(a)] = tile.T


def fill_kernel(groups, systems, near_ref, dense_ref):
    each_half(groups, systems, lambda k, h: fill(groups, k, h, True, near_ref, dense_ref))


def split_square_kernel(groups, systems, near_dense_ref, far_ref, out_ref, dense_ref):
    low = groups // 2
    share, width = far_ref.shape[1], far_ref.shape[2]

    def at(i, j=None):
        return slice(i * width, (i + 1 if j is None else j) * width)

    def square(k, h):
        dense_ref[...] = near_dense_ref[...]
        fill(groups, k, h, False, far_ref, dense_ref)
        if k == 0:
            rows, columns = (0, (h + 1) * low), (h * low, (h + 1) * low)
        else:
            rows, columns = (h * low, (h + 1) * low), (h * low, groups)
        for q in range(share):
            product = jnp.dot(
                dense_ref[q, at(*rows), :], dense_ref[q, :, at(*columns)], preferred_element_type=jnp.float32
            ).astype(jnp.bfloat16)
            for a in range(*rows):
                for b in range(max(a, columns[0]), columns[1]):
                    out_ref[place_of(groups, k, a, b)[1], q] = product[at(a - rows[0]), at(b - columns[0])]

    each_half(groups, systems, square)


def unsort_kernel(systems, slot_ref, sorted_ref, out_ref):
    spans, share = sorted_ref.shape[:2]
    stored = lax.axis_index("row") // systems <= lax.axis_index("col")

    @pl.when(stored)
    def _():
        for g in range(spans):
            for q in range(share):
                out_ref[slot_ref[g * share + q]] = sorted_ref[g, q]

    @pl.when(jnp.logical_not(stored))
    def _():
        out_ref[...] = jnp.zeros_like(out_ref)


def split_plan(own_tiles, own_index, hubs, groups, systems):
    slots, width = own_tiles.shape[0], own_tiles.shape[1]
    spans = groups * groups // 2
    share = slots // spans
    smem = pl.BlockSpec(memory_space=pltpu.SMEM)
    vmem = pl.BlockSpec(memory_space=pltpu.VMEM)
    params = pltpu.CompilerParams(vmem_limit_bytes=VMEM_LIMIT)
    region = jax.ShapeDtypeStruct(own_tiles.shape, jnp.bfloat16)
    by_group = jax.ShapeDtypeStruct((spans, share, width, width), jnp.bfloat16)

    staged = pl.pallas_call(
        stage_kernel,
        out_shape=region,
        in_specs=[vmem],
        out_specs=vmem,
        compiler_params=params,
        cost_estimate=pl.CostEstimate(flops=0, bytes_accessed=4 * own_tiles.size, transcendentals=0),
        name="stage_tiles",
    )(own_tiles)

    by_label, slot = pl.pallas_call(
        functools.partial(sort_kernel, groups, systems, len(hubs)),
        out_shape=[by_group, jax.ShapeDtypeStruct((slots,), jnp.int32)],
        in_specs=[smem] * (1 + len(hubs)) + [vmem],
        out_specs=[vmem, smem],
        scratch_shapes=[pltpu.SMEM((slots,), jnp.int32)],
        compiler_params=params,
        name="sort_by_chain",
    )(own_index, *hubs, staged)

    near = swap_in_half(by_label, groups, systems)
    far = lax.ppermute(near[: spans // 2], AXES, cross_pairs(groups, systems))
    side = groups * width
    dense = jax.ShapeDtypeStruct((share, side, side), jnp.bfloat16)
    own_dense = pl.pallas_call(
        functools.partial(fill_kernel, groups, systems),
        out_shape=dense,
        in_specs=[vmem],
        out_specs=vmem,
        compiler_params=params,
        cost_estimate=pl.CostEstimate(flops=0, bytes_accessed=2 * share * side * side, transcendentals=0),
        name="lay_out_own",
    )(near)
    squares = pl.pallas_call(
        functools.partial(split_square_kernel, groups, systems),
        out_shape=by_group,
        in_specs=[vmem] * 2,
        out_specs=vmem,
        scratch_shapes=[pltpu.VMEM(dense.shape, jnp.bfloat16)],
        compiler_params=params,
        name="square_chains",
    )(own_dense, far)
    returned = swap_in_half(squares, groups, systems)

    return pl.pallas_call(
        functools.partial(unsort_kernel, systems),
        out_shape=region,
        in_specs=[smem, vmem],
        out_specs=vmem,
        compiler_params=params,
        name="back_to_slots",
    )(slot, returned)


def spread_sort_kernel(groups, systems, hubs, *refs):
    own_ref, hub_refs, tiles_ref = refs[0], refs[1 : 1 + hubs], refs[1 + hubs]
    sorted_ref, slot_ref, table = refs[2 + hubs :]
    slots = slot_ref.shape[0]
    find_slots(groups, systems, own_ref, hub_refs, table, slot_ref)

    def move(t, carry):
        sorted_ref[t] = tiles_ref[slot_ref[t]]
        return carry

    lax.fori_loop(0, slots, move, 0)


def spread_unsort_kernel(slot_ref, sorted_ref, out_ref):
    def move(t, carry):
        out_ref[slot_ref[t]] = sorted_ref[t]
        return carry

    lax.fori_loop(0, out_ref.shape[0], move, 0)


def spread_square_kernel(groups, systems, tiles_ref, out_ref, dense):
    per_owner, width = tiles_ref.shape[1], tiles_ref.shape[2]

    def piece(v, m, c):
        return (v * systems + m) * groups + c

    def at(i):
        return pl.ds(i * width if isinstance(i, int) else pl.multiple_of(i * width, width), width)

    def one_chain(m, q):
        for i in range(groups):
            dense[at(i), at(i)] = symmetric(tiles_ref[piece(i, m, i), q])
            for j in range(i + 1, groups):
                tile = tiles_ref[piece(i, m, j), q]
                dense[at(i), at(j)] = tile
                dense[at(j), at(i)] = tile.T

        def one_tile(p, carry):
            a, b = p // groups, p % groups
            total = jnp.zeros((width, width), jnp.float32)
            for s in range(STEPS):
                k = lax.rem(a + b + s, groups)
                total += jnp.dot(dense[at(a), at(k)], dense[at(k), at(b)], preferred_element_type=jnp.float32)
            out_ref[piece(a, m, b), q] = jnp.where(a <= b, total, 0.0).astype(jnp.bfloat16)
            return carry

        lax.fori_loop(0, groups * groups, one_tile, 0)

    for m in range(systems):
        for q in range(per_owner):
            one_chain(m, q)


def spread_plan(own_tiles, own_index, hubs, groups, systems):
    slots, width = own_tiles.shape[0], own_tiles.shape[1]
    devices = groups * groups * systems
    per_owner = -(-slots // devices)
    pieces = per_owner * devices
    smem = pl.BlockSpec(memory_space=pltpu.SMEM)
    vmem = pl.BlockSpec(memory_space=pltpu.VMEM)
    params = pltpu.CompilerParams(vmem_limit_bytes=VMEM_LIMIT)

    by_label, slot = pl.pallas_call(
        functools.partial(spread_sort_kernel, groups, systems, len(hubs)),
        out_shape=(
            jax.ShapeDtypeStruct((slots, width, width), jnp.bfloat16),
            jax.ShapeDtypeStruct((slots,), jnp.int32),
        ),
        in_specs=[smem] * (1 + len(hubs)) + [vmem],
        out_specs=(vmem, smem),
        scratch_shapes=[pltpu.SMEM((slots,), jnp.int32)],
        compiler_params=params,
        name="sort_by_chain",
    )(own_index, *hubs, own_tiles)

    if pieces > slots:
        by_label = jnp.concatenate([by_label, jnp.zeros((pieces - slots, width, width), jnp.bfloat16)])
    outgoing = by_label.reshape(devices, per_owner, width, width)
    chains = lax.all_to_all(outgoing, AXES, split_axis=0, concat_axis=0, tiled=True)
    squares = pl.pallas_call(
        functools.partial(spread_square_kernel, groups, systems),
        out_shape=jax.ShapeDtypeStruct(chains.shape, jnp.bfloat16),
        in_specs=[vmem],
        out_specs=vmem,
        scratch_shapes=[pltpu.VMEM((groups * width, groups * width), jnp.bfloat16)],
        compiler_params=params,
        name="square_chains",
    )(chains)
    returned = lax.all_to_all(squares, AXES, split_axis=0, concat_axis=0, tiled=True)

    return pl.pallas_call(
        spread_unsort_kernel,
        out_shape=jax.ShapeDtypeStruct((slots, width, width), jnp.bfloat16),
        in_specs=[smem, vmem],
        out_specs=vmem,
        compiler_params=params,
        name="back_to_slots",
    )(slot, returned.reshape(pieces, width, width)[:slots])


def on_device(block_tiles, block_index):
    groups = lax.axis_size("col")
    systems = lax.axis_size("row") // groups
    own_tiles = block_tiles[0, 0]
    own_index = block_index[0, 0].T
    slots = own_tiles.shape[0]
    spans = groups * groups // 2

    hubs = [lax.ppermute(own_index, AXES, hub_pairs(groups, systems, offset)) for offset in reversed(range((groups + 1) // 2))]
    whole_window = groups == STEPS and slots % spans == 0
    plan = split_plan if whole_window else spread_plan
    return plan(own_tiles, own_index, hubs, groups, systems)[None, None]


def solution(mesh):
    in_specs = (P("row", "col", None, None, None), P("row", "col", None, None))
    out_specs = P("row", "col", None, None, None)
    return jax.shard_map(
        on_device, mesh=mesh, in_specs=in_specs, out_specs=out_specs, check_vma=False
    )
```
